256 devices in a mesh: ma: 64 (over y, z_hi, x, core), af: 4 (over z_lo).
Axes of the slice: x: 4, y: 4, z: 8 (z_hi: 2, z_lo: 4; z = z_hi * 4 + z_lo), core: 2. Of those that a mesh axis runs over, the one named last changes fastest.
Arguments:
- visibilities: bfloat16 [2, 2, 4096, 32640], P(None, None, 'ma', 'af'), may hold values from -6 to 6
- pair_base: int32 [32640], P('af'), may hold values from 0 to 8191, as said below
- window_starts: int32 [64], replicated, may hold values from 0 to 4080
- beam: bfloat16 [2, 1024, 2, 32, 8192], P(None, 'ma', None, None, 'af'), may hold values from -0.046875 to 0.046875
- kl_basis: float32 [1024, 128, 128], P(('ma', 'af')), may hold values from -0.5 to 0.5
Outputs:
- kl_modes: float32 [1024, 128], P(('ma', 'af'))
The draws below stay inside these ranges and needn't reach their ends.
Inputs may be any that keep to these rules, and one draw needn't show every extreme that they name: `pair_base`: pairs in the k-th aligned block of 8160 pairs name only baselines of the k-th block of 2048 baselines, and every baseline is named by at least one pair.
All inputs are finite; a program needn't handle non-finite values.
Results may differ from the reference program's by a relative error of at most 0.0046.
Values may be sent and summed in bfloat16 or wider, within the bound.
A program may use at most 128 MiB of HBM per device.

```python
import math
import jax
import jax.numpy as jnp
from jax import lax

CH = 2
PAIRS = 32640
NBASE = 8192
TIMES = 4096
M_WIN = 1024
M_SEG = 16
NSKY = 32
NKL = 128
NSEG = 64
PAIR_DEV = 8160
BASE_DEV = 2048


def draw_pair_base(key, part):
    key = jax.random.fold_in(key, 11)
    blocks = PAIRS // PAIR_DEV

    def one_block(block_key):
        pick_key, order_key = jax.random.split(block_key)
        cover_ids = jnp.arange(BASE_DEV, dtype=jnp.int32)
        extra_ids = jax.random.randint(pick_key, (PAIR_DEV - BASE_DEV,), 0, BASE_DEV, dtype=jnp.int32)
        ordered = jnp.concatenate([cover_ids, extra_ids])
        return ordered[jax.random.permutation(order_key, PAIR_DEV)]
    local_ids = jax.vmap(one_block)(jax.random.split(key, blocks))
    offsets = (jnp.arange(blocks, dtype=jnp.int32) * BASE_DEV)[:, None]
    return (local_ids + offsets).reshape(PAIRS)


def place_ends(values, stream_key, low, high):
    place = [jax.random.randint(jax.random.fold_in(stream_key, axis), (), 0, length) for axis, length in enumerate(values.shape)]
    widest = values.shape.index(max(values.shape))
    next_to = place[:widest] + [(place[widest] + 1) % values.shape[widest]] + place[widest + 1:]
    return values.at[tuple(place)].set(low).at[tuple(next_to)].set(high)


def levels(key, shape, cuts, smallest, largest):
    gain = 1.0
    for dim, blocks in cuts:
        draws = jax.random.uniform(jax.random.fold_in(jax.random.fold_in(key, 6), dim), (blocks,), jnp.float32, smallest / len(cuts), largest / len(cuts))
        gain = gain * jnp.repeat(jnp.exp(draws), shape[dim] // blocks).reshape((-1,) + (1,) * (len(shape) - 1 - dim))
    return gain


def scatter_about(stream_key, shape, width, limit, pieces=(), kind=jnp.bfloat16):
    entries = width * jax.random.normal(stream_key, shape, jnp.float32)
    if pieces:
        entries = entries * levels(stream_key, shape, pieces, -0.22, 0.18)
    return jnp.clip(entries, -limit, limit).astype(kind)


def setup_inputs(seed: int = 0) -> dict:
    key_list = jax.random.split(jax.random.key(seed), 6)
    visibilities = scatter_about(key_list[0], (CH, 2, TIMES, PAIRS), 1.0, 6.0, ((2, 64), (3, 4)))
    pair_base = draw_pair_base(jax.random.fold_in(key_list[5], 71), 0)
    window_starts = place_ends(jax.random.randint(key_list[2], (NSEG,), 0, TIMES - M_SEG + 1), jax.random.fold_in(key_list[2], 1), 0, TIMES - M_SEG).astype(jnp.int32)
    beam = scatter_about(key_list[3], (CH, M_WIN, 2, NSKY, NBASE), (2 * NBASE) ** -0.5, 0.046875, ((1, 64), (4, 4)))
    kl_basis = scatter_about(key_list[4], (M_WIN, NKL, NKL), NKL ** -0.5, 0.5, ((0, 256),), jnp.float32)
    return dict(visibilities=visibilities, pair_base=pair_base, window_starts=window_starts, beam=beam, kl_basis=kl_basis)


TWO_PI = 2.0 * math.pi

def dft_table(window_starts, length, seg_len):
    within = lax.iota(jnp.int32, seg_len)
    mode_ids = (window_starts[:, None] + within[None, :]).reshape(-1).astype(jnp.int32)
    sample_ids = lax.iota(jnp.int32, length)
    phase = sample_ids[:, None] * mode_ids[None, :] % length
    angle = phase.astype(jnp.float32) * (TWO_PI / length)
    scale_factor = 1.0 / math.sqrt(length)
    cosine = jnp.cos(angle) * scale_factor
    sine = jnp.sin(angle) * scale_factor
    return jnp.concatenate([cosine, sine], axis=1).astype(jnp.bfloat16)

def reference(visibilities, pair_base, window_starts, beam, kl_basis):
    counts = jax.ops.segment_sum(jnp.ones((PAIRS,), jnp.float32), pair_base, num_segments=NBASE)
    planes = visibilities.reshape(CH * 2, TIMES, PAIRS)

    def compress(plane):
        totals = jax.ops.segment_sum(plane.astype(jnp.float32).T, pair_base, num_segments=NBASE)
        return (totals / counts[:, None]).astype(jnp.bfloat16)
    compressed = lax.map(compress, planes).reshape(CH, 2, NBASE, TIMES)
    dft_tab = dft_table(window_starts, TIMES, M_SEG)

    def channel_spectra(series):
        along_real = jnp.dot(series[0], dft_tab, preferred_element_type=jnp.float32)
        along_imag = jnp.dot(series[1], dft_tab, preferred_element_type=jnp.float32)
        real_part = along_real[:, :M_WIN] + along_imag[:, M_WIN:]
        imag_part = along_imag[:, :M_WIN] - along_real[:, M_WIN:]
        return jnp.stack([real_part, imag_part]).astype(jnp.bfloat16)
    spectra = lax.map(channel_spectra, compressed)

    def project(start):
        beam_block = lax.dynamic_slice_in_dim(beam, start, 64, 1).astype(jnp.float32)
        spec_block = lax.dynamic_slice_in_dim(spectra, start, 64, 3).astype(jnp.float32)
        paired = jnp.einsum('cmqsb,crbm->mcqsr', beam_block, spec_block, precision=lax.Precision.HIGHEST)
        real_sky = paired[:, :, 0, :, 0] + paired[:, :, 1, :, 1]
        imag_sky = paired[:, :, 0, :, 1] - paired[:, :, 1, :, 0]
        vectors = jnp.stack([real_sky, imag_sky], axis=2).reshape(64, NKL)
        kl_block = lax.dynamic_slice_in_dim(kl_basis, start, 64, 0)
        return jnp.einsum('mkv,mv->mk', kl_block, vectors, precision=lax.Precision.HIGHEST)
    starts = (jnp.arange(M_WIN // 64) * 64).astype(jnp.int32)
    return lax.map(project, starts).reshape(M_WIN, NKL)
```

```python
import functools
import math

import jax
import jax.numpy as jnp
from jax import lax
from jax.experimental import pallas as pl
from jax.experimental.pallas import tpu as pltpu
from jax.sharding import PartitionSpec as P

MESH = pl.DeviceIdType.MESH
F32 = jnp.float32
BF16 = jnp.bfloat16

TIMES = 4096
SEG = 16
SEGS = 64
PAIRS = 8160
PADDED = 8192
WHOLE = 7936
BASES = 2048
T_BLK = 64
HALF = 32
B_BLK = 128
CHUNK = 256
NT = (((1,), (1,)), ((), ()))


def to_ma(half, g):
    return (g // 8) * 16 + half * 8 + g % 8


def sincos(phase):
    quadrant = (phase + 512) >> 10
    x = (phase - (quadrant << 10)).astype(F32) * (2.0 * math.pi / TIMES)
    x2 = x * x
    s = x * (1.0 + x2 * (-1.0 / 6 + x2 * (1.0 / 120 + x2 * (-1.0 / 5040 + x2 * (1.0 / 362880)))))
    c = 1.0 + x2 * (-0.5 + x2 * (1.0 / 24 + x2 * (-1.0 / 720 + x2 * (1.0 / 40320))))
    odd = (quadrant & 1) == 1
    cos = jnp.where(odd, s, c)
    sin = jnp.where(odd, c, s)
    cos = jnp.where(((quadrant + 1) & 2) == 2, -cos, cos)
    sin = jnp.where((quadrant & 2) == 2, -sin, sin)
    return cos, sin


def kernel(
    starts, ids, kl, vis_hbm, beam_hbm, out,
    vis, tail, beam, local, counts, table, s1, r1, s2, r2, weights, total, v_send, v_recv,
    vis_sem, beam_sem, ss1, rs1, ss2, rs2, z_sem, ssv, rsv,
):
    ma = lax.axis_index("ma")
    af = lax.axis_index("af")
    y = ma // 16
    half = (ma // 8) % 2
    g = y * 8 + ma % 8
    partner = to_ma(1 - half, g)

    vis_copy = pltpu.make_async_copy(vis_hbm, vis, vis_sem)
    vis_copy.start()
    beam_copy = pltpu.make_async_copy(beam_hbm, beam, beam_sem)
    beam_copy.start()

    barrier = pltpu.get_barrier_semaphore()
    pl.semaphore_signal(barrier, inc=1, device_id=(partner, af), device_id_type=MESH)

    def greet(k, _):
        pl.semaphore_signal(barrier, inc=1, device_id=(to_ma(half, lax.rem(g + k, HALF)), af), device_id_type=MESH)
        return 0

    lax.fori_loop(1, HALF, greet, 0)

    def greet_af(k, _):
        pl.semaphore_signal(barrier, inc=1, device_id=(ma, lax.rem(af + k, 4)), device_id_type=MESH)
        return 0

    lax.fori_loop(1, 4, greet_af, 0)

    local[...] = jnp.full(local.shape, -1, jnp.int32)
    local[:, pl.ds(0, PAIRS)] = ids[...] - af * BASES
    here = local[...]
    high = (here >> 7).astype(F32)
    low = (here & 127).astype(F32)
    rows_hi = lax.broadcasted_iota(jnp.int32, (16, PADDED), 0).astype(F32)
    rows_lo = lax.broadcasted_iota(jnp.int32, (B_BLK, PADDED), 0).astype(F32)
    one_hi = jnp.where(rows_hi == jnp.broadcast_to(high, (16, PADDED)), 1.0, 0.0).astype(BF16)
    one_lo = jnp.where(rows_lo == jnp.broadcast_to(low, (B_BLK, PADDED)), 1.0, 0.0).astype(BF16)
    counts[...] = lax.dot_general(one_hi, one_lo, NT, preferred_element_type=F32)

    weights[...] = jnp.zeros(weights.shape, BF16)
    v_send[...] = jnp.zeros(v_send.shape, F32)

    vis_copy.wait()
    tail[...] = jnp.zeros(tail.shape, BF16)
    tail[:, pl.ds(0, PAIRS - WHOLE)] = vis[:, pl.ds(WHOLE, PAIRS - WHOLE)]

    def compress(j):
        start = j * CHUNK
        wanted = local[...] - start
        wanted = jnp.where((wanted >= 0) & (wanted < CHUNK), wanted, -1).astype(BF16)
        rows = lax.broadcasted_iota(jnp.int32, (CHUNK, PADDED), 0).astype(BF16)
        one = jnp.where(rows == jnp.broadcast_to(wanted, (CHUNK, PADDED)), BF16(1), BF16(0))
        sums = lax.dot_general(vis[:, pl.ds(0, WHOLE)], one[:, :WHOLE], NT, preferred_element_type=F32)
        sums += lax.dot_general(tail[...], one[:, WHOLE:], NT, preferred_element_type=F32)
        for h in range(2):
            scale = 1.0 / counts[pl.ds(j * 2 + h, 1), :]
            for c in range(2):
                for r in range(2):
                    piece = sums[(c * 2 + r) * T_BLK : (c * 2 + r + 1) * T_BLK, h * B_BLK : (h + 1) * B_BLK]
                    s1[j * 4 + h * 2 + c, :, r * B_BLK : (r + 1) * B_BLK] = (piece * scale).astype(BF16)

    def send_block(d):
        @pl.when(d == g)
        def _():
            pltpu.make_async_copy(s1.at[d], r1.at[d], rs1.at[y]).start()

        @pl.when(d != g)
        def _():
            pltpu.make_async_remote_copy(
                src_ref=s1.at[d], dst_ref=r1.at[g], send_sem=ss1, recv_sem=rs1.at[y],
                device_id=(to_ma(half, d), af), device_id_type=MESH,
            ).start()

    first = g // 4

    def send_chunk(j):
        def one(k, _):
            send_block(j * 4 + k)
            return 0

        lax.fori_loop(0, 4, one, 0)

    compress(first)
    pl.semaphore_wait(barrier, HALF - 1 + 1 + 3)
    pl.semaphore_signal(z_sem, inc=1, device_id=(partner, af), device_id_type=MESH)
    send_chunk(first)

    def chunk_step(k, _):
        j = lax.rem(first + k, 8)
        compress(j)
        send_chunk(j)
        return 0

    lax.fori_loop(1, 8, chunk_step, 0)

    lanes = lax.broadcasted_iota(jnp.int32, (SEG, 128), 1)
    within = lax.broadcasted_iota(jnp.int32, (SEG, 128), 0)
    blk_time = (lanes // 4) * 1024 + half * 512 + (lanes % 4) * 128

    def table_step(s, _):
        mode = starts[s] + within
        base_c, base_s = sincos((lanes * mode) & (TIMES - 1))
        base_c = base_c * (1.0 / math.sqrt(TIMES))
        base_s = base_s * (1.0 / math.sqrt(TIMES))
        blk_c, blk_s = sincos((blk_time * mode) & (TIMES - 1))
        row = pl.multiple_of(s * SEG, SEG)
        for b in range(16):
            c = jnp.broadcast_to(blk_c[:, b : b + 1], (SEG, 128))
            d = jnp.broadcast_to(blk_s[:, b : b + 1], (SEG, 128))
            table[pl.ds(row, SEG), b * 128 : (b + 1) * 128] = (base_c * c - base_s * d).astype(BF16)
            table[pl.ds(row + SEGS * SEG, SEG), b * 128 : (b + 1) * 128] = (base_s * c + base_c * d).astype(BF16)
        return 0

    lax.fori_loop(0, SEGS, table_step, 0)

    for q in range(4):
        part = r1.at[pl.ds(q * 8, 8)]
        pltpu.make_async_copy(part, part, rs1.at[q]).wait()
    pl.semaphore_wait(z_sem, 1)

    def transform_step(k, _):
        tile = lax.rem(y + k, 4)
        row = pl.multiple_of(tile * 256, 256)
        series = r1[...].reshape(HALF * T_BLK, 2 * B_BLK)
        along_cos = jnp.dot(table[pl.ds(row, 256), :], series, preferred_element_type=F32)
        along_sin = jnp.dot(table[pl.ds(row + 1024, 256), :], series, preferred_element_type=F32)
        real = along_cos[:, :B_BLK] + along_sin[:, B_BLK:]
        imag = along_cos[:, B_BLK:] - along_sin[:, :B_BLK]
        s2[pl.ds(tile * 16, 16), :, 0:B_BLK] = real.astype(BF16).reshape(16, SEG, B_BLK)
        s2[pl.ds(tile * 16, 16), :, B_BLK : 2 * B_BLK] = imag.astype(BF16).reshape(16, SEG, B_BLK)

        def send(i, _):
            d = tile * 16 + lax.rem(i + (1 - half) * 8, 16)

            @pl.when(d == ma)
            def _():
                pltpu.make_async_copy(s2.at[d], r2.at[d], rs2.at[y]).start()

            @pl.when(d != ma)
            def _():
                pltpu.make_async_remote_copy(
                    src_ref=s2.at[d], dst_ref=r2.at[ma], send_sem=ss2, recv_sem=rs2.at[y],
                    device_id=(d, af), device_id_type=MESH,
                ).start()

            return 0

        lax.fori_loop(0, 16, send, 0)
        return 0

    lax.fori_loop(0, 4, transform_step, 0)

    beam_copy.wait()

    def project_step(k, _):
        q = lax.rem(y - k + 4, 4)
        part = r2.at[pl.ds(q * 16, 16)]
        pltpu.make_async_copy(part, part, rs2.at[q]).wait()
        for c in range(2):
            for h in range(2):
                for x in range(4):
                    block = r2[q * 16 + h * 8 + x * 2 + c]
                    for r in range(2):
                        weights[c, (h * 2 + r) * SEG : (h * 2 + r + 1) * SEG, x * B_BLK : (x + 1) * B_BLK] = block[:, r * B_BLK : (r + 1) * B_BLK]
        column = pl.multiple_of(q * 512, 512)
        for c in range(2):
            got = lax.dot_general(beam[c, :, pl.ds(column, 512)], weights[c], NT, preferred_element_type=F32)

            @pl.when(k == 0)
            def _():
                total[c] = got

            @pl.when(k != 0)
            def _():
                total[c] += got

        return 0

    lax.fori_loop(0, 4, project_step, 0)

    lane = lax.broadcasted_iota(jnp.int32, (32, 128), 1)
    is_real = ((lane >> 4) & 1) == 0
    pieces = []
    for c in range(2):
        own = []
        for q in range(2):
            kept = jnp.zeros((32, 128), F32)
            for m in range(SEG):
                kept = jnp.where((lane & 15) == m, total[c, m * 64 + q * 32 : m * 64 + (q + 1) * 32, :], kept)
            own.append(kept)
        pieces.append(jnp.where(is_real, own[0], own[1]))
        pieces.append(jnp.where(is_real, -own[1], own[0]))
    turned = jnp.concatenate(pieces, axis=0).T
    sky = turned[0:16] + turned[16:32] + turned[32:48] + turned[48:64]
    for a in range(4):
        v_send[a, 0:4, :] = sky[a * 4 : a * 4 + 4]
    pltpu.make_async_copy(v_send.at[af], v_recv.at[af], rsv).start()

    def send_sky(k, _):
        a = lax.rem(af + k, 4)
        pltpu.make_async_remote_copy(
            src_ref=v_send.at[a], dst_ref=v_recv.at[af], send_sem=ssv, recv_sem=rsv,
            device_id=(ma, a), device_id_type=MESH,
        ).start()
        return 0

    lax.fori_loop(1, 4, send_sky, 0)
    pltpu.make_async_copy(v_recv, v_recv, rsv).wait()
    vectors = v_recv[0] + v_recv[1] + v_recv[2] + v_recv[3]
    for m in range(4):
        product = kl[m] * jnp.broadcast_to(vectors[m : m + 1, :], (128, 128))
        out[m : m + 1, :] = jnp.sum(product.T, axis=0, keepdims=True)

    sent = s1.at[pl.ds(0, HALF - 1)]
    pltpu.make_async_copy(sent, sent, ss1).wait()
    sent = s2.at[pl.ds(0, SEGS - 1)]
    pltpu.make_async_copy(sent, sent, ss2).wait()
    sent = v_send.at[pl.ds(0, 3)]
    pltpu.make_async_copy(sent, sent, ssv).wait()


def body(visibilities, pair_base, window_starts, beam, kl_basis):
    vis = visibilities.reshape(4 * T_BLK, PAIRS)
    rows = beam.reshape(2, SEG * 64, BASES)
    vmem = pl.BlockSpec(memory_space=pltpu.VMEM)
    return pl.pallas_call(
        kernel,
        out_shape=jax.ShapeDtypeStruct((4, 128), F32),
        in_specs=[
            pl.BlockSpec(memory_space=pltpu.SMEM),
            vmem,
            vmem,
            pl.BlockSpec(memory_space=pl.ANY),
            pl.BlockSpec(memory_space=pl.ANY),
        ],
        out_specs=vmem,
        scratch_shapes=[
            pltpu.VMEM((4 * T_BLK, PAIRS), BF16),
            pltpu.VMEM((4 * T_BLK, PADDED - WHOLE), BF16),
            pltpu.VMEM((2, SEG * 64, BASES), BF16),
            pltpu.VMEM((1, PADDED), jnp.int32),
            pltpu.VMEM((16, B_BLK), F32),
            pltpu.VMEM((2 * SEGS * SEG, HALF * T_BLK), BF16),
            pltpu.VMEM((HALF, T_BLK, 2 * B_BLK), BF16),
            pltpu.VMEM((HALF, T_BLK, 2 * B_BLK), BF16),
            pltpu.VMEM((SEGS, SEG, 2 * B_BLK), BF16),
            pltpu.VMEM((SEGS, SEG, 2 * B_BLK), BF16),
            pltpu.VMEM((2, 128, 512), BF16),
            pltpu.VMEM((2, SEG * 64, 128), F32),
            pltpu.VMEM((4, 8, 128), F32),
            pltpu.VMEM((4, 8, 128), F32),
            pltpu.SemaphoreType.DMA,
            pltpu.SemaphoreType.DMA,
            pltpu.SemaphoreType.DMA,
            pltpu.SemaphoreType.DMA((4,)),
            pltpu.SemaphoreType.DMA,
            pltpu.SemaphoreType.DMA((4,)),
            pltpu.SemaphoreType.REGULAR,
            pltpu.SemaphoreType.DMA,
            pltpu.SemaphoreType.DMA,
        ],
        compiler_params=pltpu.CompilerParams(
            collective_id=0, has_side_effects=True, vmem_limit_bytes=56 * 2**20
        ),
    )(window_starts, pair_base.reshape(1, PAIRS), kl_basis, vis, rows)


def solution(mesh):
    in_specs = (
        P(None, None, "ma", "af"),
        P("af"),
        P(),
        P(None, "ma", None, None, "af"),
        P(("ma", "af"), None, None),
    )
    out_specs = P(("ma", "af"), None)
    return jax.shard_map(body, mesh=mesh, in_specs=in_specs, out_specs=out_specs, check_vma=False)
```

```python
import math

import jax
import jax.numpy as jnp
from jax import lax
from jax.experimental import pallas as pl
from jax.experimental.pallas import tpu as pltpu
from jax.sharding import PartitionSpec as P

MESH = pl.DeviceIdType.MESH
F32 = jnp.float32
BF16 = jnp.bfloat16

TIMES = 4096
SEG = 16
SEGS = 64
PAIRS = 8160
PADDED = 8192
WHOLE = 7936
BASES = 2048
T_BLK = 64
HALF = 32
B_BLK = 64
CHUNK = 256
OFFSETS = (
    ((2, 1), (2, 3), (1, 2), (3, 2)),
    ((2, 0), (0, 2), (1, 1), (3, 3)),
    ((1, 3), (3, 1), (2, 2), (1, 0)),
    ((0, 1), (3, 0), (0, 3), (0, 0)),
)
NT = (((1,), (1,)), ((), ()))


def to_ma(half, g):
    return (g // 8) * 16 + half * 8 + g % 8


def sincos(phase):
    quadrant = (phase + 512) >> 10
    x = (phase - (quadrant << 10)).astype(F32) * (2.0 * math.pi / TIMES)
    x2 = x * x
    s = x * (1.0 + x2 * (-1.0 / 6 + x2 * (1.0 / 120 + x2 * (-1.0 / 5040 + x2 * (1.0 / 362880)))))
    c = 1.0 + x2 * (-0.5 + x2 * (1.0 / 24 + x2 * (-1.0 / 720 + x2 * (1.0 / 40320))))
    odd = (quadrant & 1) == 1
    cos = jnp.where(odd, s, c)
    sin = jnp.where(odd, c, s)
    cos = jnp.where(((quadrant + 1) & 2) == 2, -cos, cos)
    sin = jnp.where((quadrant & 2) == 2, -sin, sin)
    return cos, sin


def kernel(
    starts, ids, kl, vis_hbm, beam_hbm, out,
    vis, tail, beam, high, low, counts, table, s1, r1, s2, r2, series, halves, weights, total, turned_kl, v_send, v_recv,
    vis_sem, beam_sem, ss1, rs1, ss2, rs2, z_sem, ssv, rsv,
):
    ma = lax.axis_index("ma")
    af = lax.axis_index("af")
    y = ma // 16
    half = (ma // 8) % 2
    g = y * 8 + ma % 8
    x = (g // 2) % 4
    partner = to_ma(1 - half, g)

    vis_copy = pltpu.make_async_copy(vis_hbm, vis, vis_sem)
    vis_copy.start()

    barrier = pltpu.get_barrier_semaphore()
    pl.semaphore_signal(barrier, inc=1, device_id=(partner, af), device_id_type=MESH)

    def greet(k, _):
        pl.semaphore_signal(barrier, inc=1, device_id=(to_ma(half, lax.rem(g + k, HALF)), af), device_id_type=MESH)
        return 0

    lax.fori_loop(1, HALF, greet, 0)

    def greet_af(k, _):
        pl.semaphore_signal(barrier, inc=1, device_id=(ma, lax.rem(af + k, 4)), device_id_type=MESH)
        return 0

    lax.fori_loop(1, 4, greet_af, 0)

    high[...] = jnp.full(high.shape, -1, jnp.int32)
    low[...] = jnp.zeros(low.shape, F32)
    local = ids[...] - af * BASES
    high[:, pl.ds(0, PAIRS)] = local >> 6
    low[:, pl.ds(0, PAIRS)] = (local & 63).astype(F32)
    rows_hi = lax.broadcasted_iota(jnp.int32, (32, PADDED), 0)
    rows_lo = (lax.broadcasted_iota(jnp.int32, (2 * B_BLK, PADDED), 0) & (B_BLK - 1)).astype(BF16)
    one_hi = jnp.where(rows_hi == jnp.broadcast_to(high[...], (32, PADDED)), 1.0, 0.0).astype(BF16)
    one_lo = jnp.where(rows_lo == jnp.broadcast_to(low[...].astype(BF16), (2 * B_BLK, PADDED)), BF16(1), BF16(0))
    counts[...] = lax.dot_general(one_hi, one_lo, NT, preferred_element_type=F32)

    lanes = lax.broadcasted_iota(jnp.int32, (SEG, 128), 1)
    within = lax.broadcasted_iota(jnp.int32, (SEG, 128), 0)

    def table_step(step):
        k = step // 16
        tile = step % 16
        start = jnp.full((SEG, 128), 0, jnp.int32)
        for w in range(4):
            start = jnp.where((within >> 2) == w, starts[tile * 4 + w], start)
        mode = start + ((k - start) & 3) + 4 * (within & 3)
        cos, sin = sincos(((lanes + half * 512) * mode) & (TIMES - 1))
        cos = cos * (1.0 / math.sqrt(TIMES))
        sin = sin * (1.0 / math.sqrt(TIMES))
        step_c, step_s = sincos((128 * mode) & (TIMES - 1))
        row = pl.multiple_of(tile * SEG, SEG)
        for b in range(4):
            table[k, pl.ds(row, SEG), b * 128 : (b + 1) * 128] = cos.astype(BF16)
            table[k, pl.ds(row + 256, SEG), b * 128 : (b + 1) * 128] = sin.astype(BF16)
            if b < 3:
                cos, sin = cos * step_c - sin * step_s, sin * step_c + cos * step_s

    def table_steps(i, _):
        for w in range(4):
            table_step(i * 4 + w)
        return 0

    lax.fori_loop(0, 16, table_steps, 0)

    vis_copy.wait()
    beam_copy = pltpu.make_async_copy(beam_hbm, beam, beam_sem)
    beam_copy.start()
    tail[...] = jnp.zeros(tail.shape, BF16)
    tail[:, pl.ds(0, PAIRS - WHOLE)] = vis[:, pl.ds(WHOLE, PAIRS - WHOLE)]

    lane = lax.broadcasted_iota(jnp.int32, (1, 128), 1)
    left = lane < B_BLK

    def chunk_step(k, _):
        batch = k // 4
        n = k % 4
        chips = []
        for sub in range(4):
            dx = dy = 0
            for i in range(4):
                dx = jnp.where(n == i, OFFSETS[i][sub][0], dx)
                dy = jnp.where(n == i, OFFSETS[i][sub][1], dy)
            chips.append(lax.rem(y + dy, 4) * 4 + lax.rem(x + dx, 4))
        wanted = jnp.full((1, PADDED), -1.0, F32)
        for sub in range(4):
            wanted = jnp.where(high[...] == batch * 16 + chips[sub], low[...] + (sub * B_BLK), wanted)
        rows = lax.broadcasted_iota(jnp.int32, (CHUNK, PADDED), 0).astype(BF16)
        one = jnp.where(rows == jnp.broadcast_to(wanted.astype(BF16), (CHUNK, PADDED)), BF16(1), BF16(0))
        sums = lax.dot_general(vis[:, pl.ds(0, WHOLE)], one[:, :WHOLE], NT, preferred_element_type=F32)
        sums += lax.dot_general(tail[...], one[:, WHOLE:], NT, preferred_element_type=F32)
        for pair in range(2):
            near, far = chips[pair * 2], chips[pair * 2 + 1]
            scale = 1.0 / jnp.where(left, counts[pl.ds(batch * 16 + near, 1), :], counts[pl.ds(batch * 16 + far, 1), :])
            for c in range(2):
                real = sums[c * 128 : c * 128 + T_BLK, pair * 128 : (pair + 1) * 128] * scale
                imag = sums[c * 128 + T_BLK : (c + 1) * 128, pair * 128 : (pair + 1) * 128] * scale
                s1[batch, near * 2 + c] = jnp.where(left, real, pltpu.roll(imag, B_BLK, 1)).astype(BF16)
                s1[batch, far * 2 + c] = jnp.where(left, pltpu.roll(real, B_BLK, 1), imag).astype(BF16)

        @pl.when(k == 0)
        def _():
            pl.semaphore_wait(barrier, HALF - 1 + 1 + 3)
            pl.semaphore_signal(z_sem, inc=1, device_id=(partner, af), device_id_type=MESH)

        for sub in range(4):
            for c in range(2):
                d = chips[sub] * 2 + c

                @pl.when(d == g)
                def _():
                    pltpu.make_async_copy(s1.at[batch, d], r1.at[batch, d], rs1.at[batch]).start()

                @pl.when(d != g)
                def _():
                    pltpu.make_async_remote_copy(
                        src_ref=s1.at[batch, d], dst_ref=r1.at[batch, g], send_sem=ss1, recv_sem=rs1.at[batch],
                        device_id=(to_ma(half, d), af), device_id_type=MESH,
                    ).start()

        return 0

    sign = jnp.where(left, 1.0, -1.0)
    upper = (lax.broadcasted_iota(jnp.int32, (1, 8, 1), 1)) < 4

    def transform(batch, _):
        part = r1.at[batch]
        pltpu.make_async_copy(part, part, rs1.at[batch]).wait()
        a = [r1[batch, q * 8 : (q + 1) * 8].reshape(8 * T_BLK, 2 * B_BLK).astype(F32) for q in range(4)]
        even, odd = a[0] + a[2], a[1] + a[3]
        series[0] = (even + odd).astype(BF16)
        series[2] = (even - odd).astype(BF16)
        even, odd = a[0] - a[2], sign * pltpu.roll(a[1] - a[3], B_BLK, 1)
        series[1] = (even + odd).astype(BF16)
        series[3] = (even - odd).astype(BF16)
        both = []
        for k in range(4):
            along = jnp.dot(table[k], series[k], preferred_element_type=F32)
            mixed = along[0:256] + sign * pltpu.roll(along[256:512], B_BLK, 1)
            both.append(mixed.reshape(32, 8, 2 * B_BLK))
        for p in range(2):
            first, second = both[2 * p], both[2 * p + 1]
            now = jnp.where(upper, first, pltpu.roll(second, 4, 1))
            later = jnp.where(upper, pltpu.roll(first, 4, 1), second)
            halves[:, 0, p * 8 : (p + 1) * 8, :] = now
            halves[:, 1, p * 8 : (p + 1) * 8, :] = later
        s2[batch] = halves[...].reshape(SEGS, SEG, 2 * B_BLK).astype(BF16)

        def send(i, _):
            d = lax.rem(y + i // 16, 4) * 16 + lax.rem(i % 16 + (1 - half) * 8, 16)

            @pl.when(d == ma)
            def _():
                pltpu.make_async_copy(s2.at[batch, d], r2.at[batch, d], rs2.at[batch, y]).start()

            @pl.when(d != ma)
            def _():
                pltpu.make_async_remote_copy(
                    src_ref=s2.at[batch, d], dst_ref=r2.at[batch, ma], send_sem=ss2, recv_sem=rs2.at[batch, y],
                    device_id=(d, af), device_id_type=MESH,
                ).start()

            return 0

        lax.fori_loop(0, SEGS, send, 0)
        return 0

    lax.fori_loop(0, 8, chunk_step, 0)
    pl.semaphore_wait(z_sem, 1)
    lax.fori_loop(0, 2, transform, 0)
    for m in range(4):
        turned_kl[m] = kl[m].T
    weights[...] = jnp.zeros(weights.shape, BF16)
    total[...] = jnp.zeros(total.shape, F32)
    v_send[...] = jnp.zeros(v_send.shape, F32)


    beam_copy.wait()

    def project_step(k, _):
        batch = k // 4
        q = lax.rem(y - k % 4 + 4, 4)
        part = r2.at[batch, pl.ds(q * 16, 16)]
        pltpu.make_async_copy(part, part, rs2.at[batch, q]).wait()
        for c in range(2):
            for h in range(2):
                for pair in range(2):
                    near = r2[batch, q * 16 + h * 8 + pair * 4 + c].astype(F32)
                    far = r2[batch, q * 16 + h * 8 + pair * 4 + 2 + c].astype(F32)
                    real = jnp.where(left, near, pltpu.roll(far, B_BLK, 1))
                    imag = jnp.where(left, pltpu.roll(near, B_BLK, 1), far)
                    weights[c, h * 2 * SEG : (h * 2 + 1) * SEG, pair * 128 : (pair + 1) * 128] = real.astype(BF16)
                    weights[c, (h * 2 + 1) * SEG : (h * 2 + 2) * SEG, pair * 128 : (pair + 1) * 128] = imag.astype(BF16)
        column = pl.multiple_of(batch * 1024 + q * 256, 256)
        for c in range(2):
            total[c] += lax.dot_general(beam[c, :, pl.ds(column, 256)], weights[c], NT, preferred_element_type=F32)
        return 0

    lax.fori_loop(0, 8, project_step, 0)

    mode_lane = lax.broadcasted_iota(jnp.int32, (32, 128), 1)
    is_real = ((mode_lane >> 4) & 1) == 0
    mode_of = ((((mode_lane >> 2) & 3) - starts[ma]) & 3) + 4 * (mode_lane & 3)
    pieces = []
    for c in range(2):
        own = []
        for q in range(2):
            kept = jnp.zeros((32, 128), F32)
            for m in range(SEG):
                kept = jnp.where(mode_of == m, total[c, m * 64 + q * 32 : m * 64 + (q + 1) * 32, :], kept)
            own.append(kept)
        pieces.append(jnp.where(is_real, own[0], own[1]))
        pieces.append(jnp.where(is_real, -own[1], own[0]))
    turned = jnp.concatenate(pieces, axis=0).T
    sky = turned[0:16] + turned[16:32] + turned[32:48] + turned[48:64]
    window = jnp.full((4, 128), 0, jnp.int32) + starts[ma]
    for i in range(4):
        kept = sky[0:4]
        for k in range(1, 4):
            kept = jnp.where(((window + i) & 3) == k, sky[k * 4 : k * 4 + 4], kept)
        for n in range(4):
            v_send[n, i : i + 1, :] = kept[n : n + 1]
    pltpu.make_async_copy(v_send.at[af], v_recv.at[af], rsv).start()

    def send_sky(k, _):
        a = lax.rem(af + k, 4)
        pltpu.make_async_remote_copy(
            src_ref=v_send.at[a], dst_ref=v_recv.at[af], send_sem=ssv, recv_sem=rsv,
            device_id=(ma, a), device_id_type=MESH,
        ).start()
        return 0

    lax.fori_loop(1, 4, send_sky, 0)
    pltpu.make_async_copy(v_recv, v_recv, rsv).wait()
    vectors = (v_recv[0] + v_recv[1] + v_recv[2] + v_recv[3]).T
    for m in range(4):
        product = turned_kl[m] * jnp.broadcast_to(vectors[:, m : m + 1], (128, 128))
        out[m : m + 1, :] = jnp.sum(product, axis=0, keepdims=True)

    sent = s1.at[:, pl.ds(0, HALF - 1)]
    pltpu.make_async_copy(sent, sent, ss1).wait()
    sent = s2.at[:, pl.ds(0, SEGS - 1)]
    pltpu.make_async_copy(sent, sent, ss2).wait()
    sent = v_send.at[pl.ds(0, 3)]
    pltpu.make_async_copy(sent, sent, ssv).wait()


def body(visibilities, pair_base, window_starts, beam, kl_basis):
    vis = visibilities.reshape(4 * T_BLK, PAIRS)
    rows = beam.reshape(2, SEG * 64, BASES)
    vmem = pl.BlockSpec(memory_space=pltpu.VMEM)
    return pl.pallas_call(
        kernel,
        out_shape=pltpu.VMEM((4, 128), F32),
        in_specs=[
            pl.BlockSpec(memory_space=pltpu.SMEM),
            vmem,
            vmem,
            pl.BlockSpec(memory_space=pl.ANY),
            pl.BlockSpec(memory_space=pl.ANY),
        ],
        out_specs=vmem,
        scratch_shapes=[
            pltpu.VMEM((4 * T_BLK, PAIRS), BF16),
            pltpu.VMEM((4 * T_BLK, PADDED - WHOLE), BF16),
            pltpu.VMEM((2, SEG * 64, BASES), BF16),
            pltpu.VMEM((1, PADDED), jnp.int32),
            pltpu.VMEM((1, PADDED), F32),
            pltpu.VMEM((32, 2 * B_BLK), F32),
            pltpu.VMEM((4, 512, 512), BF16),
            pltpu.VMEM((2, HALF, T_BLK, 2 * B_BLK), BF16),
            pltpu.VMEM((2, HALF, T_BLK, 2 * B_BLK), BF16),
            pltpu.VMEM((2, SEGS, SEG, 2 * B_BLK), BF16),
            pltpu.VMEM((2, SEGS, SEG, 2 * B_BLK), BF16),
            pltpu.VMEM((4, 512, 2 * B_BLK), BF16),
            pltpu.VMEM((SEGS // 2, 2, SEG, 2 * B_BLK), F32),
            pltpu.VMEM((2, 128, 256), BF16),
            pltpu.VMEM((2, SEG * 64, 128), F32),
            pltpu.VMEM((4, 128, 128), F32),
            pltpu.VMEM((4, 8, 128), F32),
            pltpu.VMEM((4, 8, 128), F32),
            pltpu.SemaphoreType.DMA,
            pltpu.SemaphoreType.DMA,
            pltpu.SemaphoreType.DMA,
            pltpu.SemaphoreType.DMA((2,)),
            pltpu.SemaphoreType.DMA,
            pltpu.SemaphoreType.DMA((2, 4)),
            pltpu.SemaphoreType.REGULAR,
            pltpu.SemaphoreType.DMA,
            pltpu.SemaphoreType.DMA,
        ],
        compiler_params=pltpu.CompilerParams(
            collective_id=0, has_side_effects=True, vmem_limit_bytes=56 * 2**20
        ),
    )(window_starts, pair_base.reshape(1, PAIRS), kl_basis, vis, rows)


def solution(mesh):
    in_specs = (
        P(None, None, "ma", "af"),
        P("af"),
        P(),
        P(None, "ma", None, None, "af"),
        P(("ma", "af"), None, None),
    )
    out_specs = P(("ma", "af"), None)
    return jax.shard_map(body, mesh=mesh, in_specs=in_specs, out_specs=out_specs, check_vma=False)
```

```python
import math

import jax
import jax.numpy as jnp
from jax import lax
from jax.experimental import pallas as pl
from jax.experimental.pallas import tpu as pltpu
from jax.sharding import PartitionSpec as P

MESH = pl.DeviceIdType.MESH
F32 = jnp.float32
BF16 = jnp.bfloat16

TIMES = 4096
SEG = 16
SEGS = 64
PAIRS = 8160
PADDED = 8192
WHOLE = 7936
BASES = 2048
T_BLK = 64
HALF = 32
B_BLK = 64
CHUNK = 256
OFFSETS = (
    ((2, 1), (2, 3), (1, 2), (3, 2)),
    ((2, 0), (0, 2), (1, 1), (3, 3)),
    ((1, 3), (3, 1), (2, 2), (1, 0)),
    ((0, 1), (3, 0), (0, 3), (0, 0)),
)
NT = (((1,), (1,)), ((), ()))


def to_ma(half, g):
    return (g // 8) * 16 + half * 8 + g % 8


def sincos(phase):
    quadrant = (phase + 512) >> 10
    x = (phase - (quadrant << 10)).astype(F32) * (2.0 * math.pi / TIMES)
    x2 = x * x
    s = x * (1.0 + x2 * (-1.0 / 6 + x2 * (1.0 / 120 + x2 * (-1.0 / 5040 + x2 * (1.0 / 362880)))))
    c = 1.0 + x2 * (-0.5 + x2 * (1.0 / 24 + x2 * (-1.0 / 720 + x2 * (1.0 / 40320))))
    odd = (quadrant & 1) == 1
    cos = jnp.where(odd, s, c)
    sin = jnp.where(odd, c, s)
    cos = jnp.where(((quadrant + 1) & 2) == 2, -cos, cos)
    sin = jnp.where((quadrant & 2) == 2, -sin, sin)
    return cos, sin


def kernel(
    starts, ids, kl_hbm, vis_hbm, beam_hbm, out,
    vis, tail, beam, high, low, counts, table, s1, r1, s2, r2, series, halves, weights, total, kl, turned_kl, v_send, v_recv,
    vis_sem, kl_sem, beam_sem, ss1, rs1, ss2, rs2, z_sem, ssv, rsv,
):
    ma = lax.axis_index("ma")
    af = lax.axis_index("af")
    y = ma // 16
    half = (ma // 8) % 2
    g = y * 8 + ma % 8
    x = (g // 2) % 4
    partner = to_ma(1 - half, g)

    vis_copy = pltpu.make_async_copy(vis_hbm, vis, vis_sem)
    vis_copy.start()
    kl_copy = pltpu.make_async_copy(kl_hbm, kl, kl_sem)
    kl_copy.start()

    barrier = pltpu.get_barrier_semaphore()
    pl.semaphore_signal(barrier, inc=1, device_id=(partner, af), device_id_type=MESH)

    def greet(k, _):
        pl.semaphore_signal(barrier, inc=1, device_id=(to_ma(half, lax.rem(g + k, HALF)), af), device_id_type=MESH)
        return 0

    lax.fori_loop(1, HALF, greet, 0)

    def greet_af(k, _):
        pl.semaphore_signal(barrier, inc=1, device_id=(ma, lax.rem(af + k, 4)), device_id_type=MESH)
        return 0

    lax.fori_loop(1, 4, greet_af, 0)

    high[...] = jnp.full(high.shape, -1, jnp.int32)
    low[...] = jnp.zeros(low.shape, F32)
    local = ids[...] - af * BASES
    high[:, pl.ds(0, PAIRS)] = local >> 6
    low[:, pl.ds(0, PAIRS)] = (local & 63).astype(F32)
    rows_hi = lax.broadcasted_iota(jnp.int32, (32, PADDED), 0)
    rows_lo = (lax.broadcasted_iota(jnp.int32, (2 * B_BLK, PADDED), 0) & (B_BLK - 1)).astype(BF16)
    one_hi = jnp.where(rows_hi == jnp.broadcast_to(high[...], (32, PADDED)), 1.0, 0.0).astype(BF16)
    one_lo = jnp.where(rows_lo == jnp.broadcast_to(low[...].astype(BF16), (2 * B_BLK, PADDED)), BF16(1), BF16(0))
    counts[...] = lax.dot_general(one_hi, one_lo, NT, preferred_element_type=F32)

    lanes = lax.broadcasted_iota(jnp.int32, (SEG, 128), 1)
    within = lax.broadcasted_iota(jnp.int32, (SEG, 128), 0)
    window_row = within >> 2
    first_time = lanes + half * 512
    turns = []
    for b in range(4):
        up = sincos((first_time + 128 * b) & (TIMES - 1))
        down = sincos((-3 * (first_time + 128 * b)) & (TIMES - 1))
        turns.append((up, down))

    def table_step(tile, _):
        start = jnp.full((SEG, 128), 0, jnp.int32)
        for w in range(4):
            start = jnp.where(window_row == w, starts[tile * 4 + w], start)
        mode = start + ((-start) & 3) + 4 * (within & 3)
        cos, sin = sincos((first_time * mode) & (TIMES - 1))
        cos = cos * (1.0 / math.sqrt(TIMES))
        sin = sin * (1.0 / math.sqrt(TIMES))
        step_c, step_s = sincos((128 * mode) & (TIMES - 1))
        own = jnp.where((tile // 2) % 2 == half, 1, 0)
        row = pl.multiple_of((tile // 4 * 2 + tile % 2) * SEG, SEG)
        wraps = [((k - start) & 3) == 0 for k in range(4)]
        for b in range(4):
            c, d = cos, sin
            for k in range(4):
                if k:
                    (up_c, up_s), (down_c, down_s) = turns[b]
                    turn_c = jnp.where(wraps[k], down_c, up_c)
                    turn_s = jnp.where(wraps[k], down_s, up_s)
                    c, d = c * turn_c - d * turn_s, d * turn_c + c * turn_s
                table[k, own, pl.ds(row, SEG), b * 128 : (b + 1) * 128] = c.astype(BF16)
                table[k, own, pl.ds(row + 128, SEG), b * 128 : (b + 1) * 128] = d.astype(BF16)
            if b < 3:
                cos, sin = cos * step_c - sin * step_s, sin * step_c + cos * step_s
        return 0

    lax.fori_loop(0, 16, table_step, 0)

    vis_copy.wait()
    beam_copy = pltpu.make_async_copy(beam_hbm, beam, beam_sem)
    beam_copy.start()
    tail[...] = jnp.zeros(tail.shape, BF16)
    tail[:, pl.ds(0, PAIRS - WHOLE)] = vis[:, pl.ds(WHOLE, PAIRS - WHOLE)]

    lane = lax.broadcasted_iota(jnp.int32, (1, 128), 1)
    left = lane < B_BLK

    def chunk_step(k, _):
        batch = k // 4
        n = k % 4
        chips = []
        for sub in range(4):
            dx = dy = 0
            for i in range(4):
                dx = jnp.where(n == i, OFFSETS[i][sub][0], dx)
                dy = jnp.where(n == i, OFFSETS[i][sub][1], dy)
            chips.append(lax.rem(y + dy, 4) * 4 + lax.rem(x + dx, 4))
        wanted = jnp.full((1, PADDED), -1.0, F32)
        for sub in range(4):
            wanted = jnp.where(high[...] == batch * 16 + chips[sub], low[...] + (sub * B_BLK), wanted)
        rows = lax.broadcasted_iota(jnp.int32, (CHUNK, PADDED), 0).astype(BF16)
        one = jnp.where(rows == jnp.broadcast_to(wanted.astype(BF16), (CHUNK, PADDED)), BF16(1), BF16(0))
        sums = lax.dot_general(vis[:, pl.ds(0, WHOLE)], one[:, :WHOLE], NT, preferred_element_type=F32)
        sums += lax.dot_general(tail[...], one[:, WHOLE:], NT, preferred_element_type=F32)
        for pair in range(2):
            near, far = chips[pair * 2], chips[pair * 2 + 1]
            scale = 1.0 / jnp.where(left, counts[pl.ds(batch * 16 + near, 1), :], counts[pl.ds(batch * 16 + far, 1), :])
            for c in range(2):
                real = sums[c * 128 : c * 128 + T_BLK, pair * 128 : (pair + 1) * 128] * scale
                imag = sums[c * 128 + T_BLK : (c + 1) * 128, pair * 128 : (pair + 1) * 128] * scale
                s1[batch, near * 2 + c] = jnp.where(left, real, pltpu.roll(imag, B_BLK, 1)).astype(BF16)
                s1[batch, far * 2 + c] = jnp.where(left, pltpu.roll(real, B_BLK, 1), imag).astype(BF16)

        @pl.when(k == 0)
        def _():
            pl.semaphore_wait(barrier, HALF - 1 + 1 + 3)
            pl.semaphore_signal(z_sem, inc=1, device_id=(partner, af), device_id_type=MESH)

        for sub in range(4):
            for c in range(2):
                d = chips[sub] * 2 + c

                @pl.when(d == g)
                def _():
                    pltpu.make_async_copy(s1.at[batch, d], r1.at[batch, d], rs1.at[batch]).start()

                @pl.when(d != g)
                def _():
                    pltpu.make_async_remote_copy(
                        src_ref=s1.at[batch, d], dst_ref=r1.at[batch, g], send_sem=ss1, recv_sem=rs1.at[batch],
                        device_id=(to_ma(half, d), af), device_id_type=MESH,
                    ).start()

        return 0

    sign = jnp.where(left, 1.0, -1.0)
    upper = (lax.broadcasted_iota(jnp.int32, (1, 8, 1), 1)) < 4

    def gather(batch):
        part = r1.at[batch]
        pltpu.make_async_copy(part, part, rs1.at[batch]).wait()
        a = [r1[batch, q * 8 : (q + 1) * 8].reshape(8 * T_BLK, 2 * B_BLK).astype(F32) for q in range(4)]
        even, odd = a[0] + a[2], a[1] + a[3]
        series[batch, 0] = (even + odd).astype(BF16)
        series[batch, 2] = (even - odd).astype(BF16)
        even, odd = a[0] - a[2], sign * pltpu.roll(a[1] - a[3], B_BLK, 1)
        series[batch, 1] = (even + odd).astype(BF16)
        series[batch, 3] = (even - odd).astype(BF16)

    def transform(batch, own):
        both = []
        for k in range(4):
            along = jnp.dot(table[k, own], series[batch, k], preferred_element_type=F32)
            mixed = along[0:128] + sign * pltpu.roll(along[128:256], B_BLK, 1)
            both.append(mixed.reshape(HALF // 2, 8, 2 * B_BLK))
        for p in range(2):
            first, second = both[2 * p], both[2 * p + 1]
            now = jnp.where(upper, first, pltpu.roll(second, 4, 1))
            later = jnp.where(upper, pltpu.roll(first, 4, 1), second)
            halves[:, 0, p * 8 : (p + 1) * 8, :] = now
            halves[:, 1, p * 8 : (p + 1) * 8, :] = later
        s2[batch, own] = halves[...].reshape(HALF, SEG, 2 * B_BLK).astype(BF16)

    def send_spectra(batch, own):
        def send(i, _):
            to = lax.rem(g + i, HALF)
            d = to_ma(half if own else 1 - half, to)

            @pl.when(d == ma)
            def _():
                pltpu.make_async_copy(s2.at[batch, own, to], r2.at[batch, d], rs2.at[batch, y]).start()

            @pl.when(d != ma)
            def _():
                pltpu.make_async_remote_copy(
                    src_ref=s2.at[batch, own, to], dst_ref=r2.at[batch, ma], send_sem=ss2, recv_sem=rs2.at[batch, y],
                    device_id=(d, af), device_id_type=MESH,
                ).start()

            return 0

        lax.fori_loop(0, HALF, send, 0)

    lax.fori_loop(0, 8, chunk_step, 0)
    pl.semaphore_wait(z_sem, 1)
    gather(0)
    transform(0, 0)
    send_spectra(0, 0)
    transform(0, 1)
    gather(1)
    transform(1, 0)
    send_spectra(1, 0)
    send_spectra(0, 1)
    transform(1, 1)
    send_spectra(1, 1)
    kl_copy.wait()
    for m in range(4):
        turned_kl[m] = kl[m].T
    weights[...] = jnp.zeros(weights.shape, BF16)
    total[...] = jnp.zeros(total.shape, F32)
    v_send[...] = jnp.zeros(v_send.shape, F32)


    beam_copy.wait()

    def project_step(k, _):
        batch = k // 4
        q = lax.rem(y - k % 4 + 4, 4)
        part = r2.at[batch, pl.ds(q * 16, 16)]
        pltpu.make_async_copy(part, part, rs2.at[batch, q]).wait()
        for c in range(2):
            for h in range(2):
                for pair in range(2):
                    near = r2[batch, q * 16 + h * 8 + pair * 4 + c].astype(F32)
                    far = r2[batch, q * 16 + h * 8 + pair * 4 + 2 + c].astype(F32)
                    real = jnp.where(left, near, pltpu.roll(far, B_BLK, 1))
                    imag = jnp.where(left, pltpu.roll(near, B_BLK, 1), far)
                    weights[c, h * 2 * SEG : (h * 2 + 1) * SEG, pair * 128 : (pair + 1) * 128] = real.astype(BF16)
                    weights[c, (h * 2 + 1) * SEG : (h * 2 + 2) * SEG, pair * 128 : (pair + 1) * 128] = imag.astype(BF16)
        column = pl.multiple_of(batch * 1024 + q * 256, 256)
        for c in range(2):
            total[c] += lax.dot_general(beam[c, :, pl.ds(column, 256)], weights[c], NT, preferred_element_type=F32)
        return 0

    lax.fori_loop(0, 8, project_step, 0)

    mode_lane = lax.broadcasted_iota(jnp.int32, (32, 128), 1)
    is_real = ((mode_lane >> 4) & 1) == 0
    mode_of = ((((mode_lane >> 2) & 3) - starts[ma]) & 3) + 4 * (mode_lane & 3)
    pieces = []
    for c in range(2):
        own = []
        for q in range(2):
            kept = jnp.zeros((32, 128), F32)
            for m in range(SEG):
                kept = jnp.where(mode_of == m, total[c, m * 64 + q * 32 : m * 64 + (q + 1) * 32, :], kept)
            own.append(kept)
        pieces.append(jnp.where(is_real, own[0], own[1]))
        pieces.append(jnp.where(is_real, -own[1], own[0]))
    turned = jnp.concatenate(pieces, axis=0).T
    sky = turned[0:16] + turned[16:32] + turned[32:48] + turned[48:64]
    window = jnp.full((4, 128), 0, jnp.int32) + starts[ma]
    for i in range(4):
        kept = sky[0:4]
        for k in range(1, 4):
            kept = jnp.where(((window + i) & 3) == k, sky[k * 4 : k * 4 + 4], kept)
        for n in range(4):
            v_send[n, i : i + 1, :] = kept[n : n + 1]
    pltpu.make_async_copy(v_send.at[af], v_recv.at[af], rsv).start()

    def send_sky(k, _):
        a = lax.rem(af + k, 4)
        pltpu.make_async_remote_copy(
            src_ref=v_send.at[a], dst_ref=v_recv.at[af], send_sem=ssv, recv_sem=rsv,
            device_id=(ma, a), device_id_type=MESH,
        ).start()
        return 0

    lax.fori_loop(1, 4, send_sky, 0)
    pltpu.make_async_copy(v_recv, v_recv, rsv).wait()
    vectors = (v_recv[0] + v_recv[1] + v_recv[2] + v_recv[3]).T
    for m in range(4):
        product = turned_kl[m] * jnp.broadcast_to(vectors[:, m : m + 1], (128, 128))
        out[m : m + 1, :] = jnp.sum(product, axis=0, keepdims=True)

    sent = s1.at[:, pl.ds(0, HALF - 1)]
    pltpu.make_async_copy(sent, sent, ss1).wait()
    for sent in (s2.at[:, 0], s2.at[:, 1, pl.ds(0, HALF - 1)]):
        pltpu.make_async_copy(sent, sent, ss2).wait()
    sent = v_send.at[pl.ds(0, 3)]
    pltpu.make_async_copy(sent, sent, ssv).wait()


def body(visibilities, pair_base, window_starts, beam, kl_basis):
    vis = visibilities.reshape(4 * T_BLK, PAIRS)
    rows = beam.reshape(2, SEG * 64, BASES)
    vmem = pl.BlockSpec(memory_space=pltpu.VMEM)
    return pl.pallas_call(
        kernel,
        out_shape=pltpu.VMEM((4, 128), F32),
        in_specs=[
            pl.BlockSpec(memory_space=pltpu.SMEM),
            vmem,
            pl.BlockSpec(memory_space=pl.ANY),
            pl.BlockSpec(memory_space=pl.ANY),
            pl.BlockSpec(memory_space=pl.ANY),
        ],
        out_specs=vmem,
        scratch_shapes=[
            pltpu.VMEM((4 * T_BLK, PAIRS), BF16),
            pltpu.VMEM((4 * T_BLK, PADDED - WHOLE), BF16),
            pltpu.VMEM((2, SEG * 64, BASES), BF16),
            pltpu.VMEM((1, PADDED), jnp.int32),
            pltpu.VMEM((1, PADDED), F32),
            pltpu.VMEM((32, 2 * B_BLK), F32),
            pltpu.VMEM((4, 2, 256, 512), BF16),
            pltpu.VMEM((2, HALF, T_BLK, 2 * B_BLK), BF16),
            pltpu.VMEM((2, HALF, T_BLK, 2 * B_BLK), BF16),
            pltpu.VMEM((2, 2, HALF, SEG, 2 * B_BLK), BF16),
            pltpu.VMEM((2, SEGS, SEG, 2 * B_BLK), BF16),
            pltpu.VMEM((2, 4, 512, 2 * B_BLK), BF16),
            pltpu.VMEM((HALF // 2, 2, SEG, 2 * B_BLK), F32),
            pltpu.VMEM((2, 128, 256), BF16),
            pltpu.VMEM((2, SEG * 64, 128), F32),
            pltpu.VMEM((4, 128, 128), F32),
            pltpu.VMEM((4, 128, 128), F32),
            pltpu.VMEM((4, 8, 128), F32),
            pltpu.VMEM((4, 8, 128), F32),
            pltpu.SemaphoreType.DMA,
            pltpu.SemaphoreType.DMA,
            pltpu.SemaphoreType.DMA,
            pltpu.SemaphoreType.DMA,
            pltpu.SemaphoreType.DMA((2,)),
            pltpu.SemaphoreType.DMA,
            pltpu.SemaphoreType.DMA((2, 4)),
            pltpu.SemaphoreType.REGULAR,
            pltpu.SemaphoreType.DMA,
            pltpu.SemaphoreType.DMA,
        ],
        compiler_params=pltpu.CompilerParams(
            collective_id=0, has_side_effects=True, vmem_limit_bytes=56 * 2**20
        ),
    )(window_starts, pair_base.reshape(1, PAIRS), kl_basis, vis, rows)


def solution(mesh):
    in_specs = (
        P(None, None, "ma", "af"),
        P("af"),
        P(),
        P(None, "ma", None, None, "af"),
        P(("ma", "af"), None, None),
    )
    out_specs = P(("ma", "af"), None)
    return jax.shard_map(body, mesh=mesh, in_specs=in_specs, out_specs=out_specs, check_vma=False)
```

```python
import math

import jax
import jax.numpy as jnp
from jax import lax
from jax.experimental import pallas as pl
from jax.experimental.pallas import tpu as pltpu
from jax.sharding import PartitionSpec as P

MESH = pl.DeviceIdType.MESH
F32 = jnp.float32
BF16 = jnp.bfloat16

TIMES = 4096
SEG = 16
SEGS = 64
PAIRS = 8160
PADDED = 8192
WHOLE = 7936
BASES = 2048
T_BLK = 64
HALF = 32
B_BLK = 64
CHUNK = 256
OFFSETS = (
    ((2, 1), (2, 3), (1, 2), (3, 2)),
    ((2, 0), (0, 2), (1, 1), (3, 3)),
    ((1, 3), (3, 1), (2, 2), (1, 0)),
    ((0, 1), (3, 0), (0, 3), (0, 0)),
)
NT = (((1,), (1,)), ((), ()))


def wrap(value, size):
    return jnp.where(value >= size, value - size, value)


def sincos(phase):
    quadrant = (phase + 512) >> 10
    x = (phase - (quadrant << 10)).astype(F32) * (2.0 * math.pi / TIMES)
    x2 = x * x
    s = x * (1.0 + x2 * (-1.0 / 6 + x2 * (1.0 / 120 + x2 * (-1.0 / 5040 + x2 * (1.0 / 362880)))))
    c = 1.0 + x2 * (-0.5 + x2 * (1.0 / 24 + x2 * (-1.0 / 720 + x2 * (1.0 / 40320))))
    odd = (quadrant & 1) == 1
    cos = jnp.where(odd, s, c)
    sin = jnp.where(odd, c, s)
    cos = jnp.where(((quadrant + 1) & 2) == 2, -cos, cos)
    sin = jnp.where((quadrant & 2) == 2, -sin, sin)
    return cos, sin


def kernel(
    starts, ids, kl_hbm, vis_hbm, beam_hbm, out,
    vis, tail, beam, high, low, counts, table, s1, r1, s2, r2, series, halves, weights, total, kl, turned_kl, v_send, v_recv,
    vis_sem, kl_sem, beam_sem, ss1, rs1, ss2, rs2, z_sem, ssv, rsv,
):
    ma = lax.axis_index("ma")
    af = lax.axis_index("af")
    y = ma // 16
    half = (ma // 8) % 2
    place = ma % 8
    g = y * 8 + place
    x = place // 2
    partner = ma + 8 - 16 * half

    vis_copy = pltpu.make_async_copy(vis_hbm, vis, vis_sem)
    vis_copy.start()
    kl_copy = pltpu.make_async_copy(kl_hbm, kl, kl_sem)
    kl_copy.start()

    barrier = pltpu.get_barrier_semaphore()
    pl.semaphore_signal(barrier, inc=1, device_id=(partner, af), device_id_type=MESH)

    for dy in range(4):

        def greet(k, _, base=wrap(y + dy, 4) * 16 + half * 8):
            pl.semaphore_signal(barrier, inc=1, device_id=(base + wrap(place + k, 8), af), device_id_type=MESH)
            return 0

        lax.fori_loop(0 if dy else 1, 8, greet, 0)

    def greet_af(k, _):
        pl.semaphore_signal(barrier, inc=1, device_id=(ma, wrap(af + k, 4)), device_id_type=MESH)
        return 0

    lax.fori_loop(1, 4, greet_af, 0)

    high[...] = jnp.full(high.shape, -1, jnp.int32)
    low[...] = jnp.zeros(low.shape, F32)
    local = ids[...] - af * BASES
    high[:, pl.ds(0, PAIRS)] = local >> 6
    low[:, pl.ds(0, PAIRS)] = (local & 63).astype(F32)
    rows_hi = lax.broadcasted_iota(jnp.int32, (32, PADDED), 0)
    rows_lo = (lax.broadcasted_iota(jnp.int32, (2 * B_BLK, PADDED), 0) & (B_BLK - 1)).astype(BF16)
    one_hi = jnp.where(rows_hi == jnp.broadcast_to(high[...], (32, PADDED)), 1.0, 0.0).astype(BF16)
    one_lo = jnp.where(rows_lo == jnp.broadcast_to(low[...].astype(BF16), (2 * B_BLK, PADDED)), BF16(1), BF16(0))
    counts[...] = lax.dot_general(one_hi, one_lo, NT, preferred_element_type=F32)

    lanes = lax.broadcasted_iota(jnp.int32, (SEG, 128), 1)
    within = lax.broadcasted_iota(jnp.int32, (SEG, 128), 0)
    window_row = within >> 2
    first_time = lanes + half * 512
    turns = []
    for b in range(4):
        up = sincos((first_time + 128 * b) & (TIMES - 1))
        down = sincos((-3 * (first_time + 128 * b)) & (TIMES - 1))
        turns.append((up, down))

    def table_step(tile, _):
        start = jnp.full((SEG, 128), 0, jnp.int32)
        for w in range(4):
            start = jnp.where(window_row == w, starts[tile * 4 + w], start)
        mode = start + ((-start) & 3) + 4 * (within & 3)
        cos, sin = sincos((first_time * mode) & (TIMES - 1))
        cos = cos * (1.0 / math.sqrt(TIMES))
        sin = sin * (1.0 / math.sqrt(TIMES))
        step_c, step_s = sincos((128 * mode) & (TIMES - 1))
        own = jnp.where((tile // 2) % 2 == half, 1, 0)
        row = pl.multiple_of((tile // 4 * 2 + tile % 2) * SEG, SEG)
        wraps = [((k - start) & 3) == 0 for k in range(4)]
        for b in range(4):
            c, d = cos, sin
            for k in range(4):
                if k:
                    (up_c, up_s), (down_c, down_s) = turns[b]
                    turn_c = jnp.where(wraps[k], down_c, up_c)
                    turn_s = jnp.where(wraps[k], down_s, up_s)
                    c, d = c * turn_c - d * turn_s, d * turn_c + c * turn_s
                table[k, own, pl.ds(row, SEG), b * 128 : (b + 1) * 128] = c.astype(BF16)
                table[k, own, pl.ds(row + 128, SEG), b * 128 : (b + 1) * 128] = d.astype(BF16)
            if b < 3:
                cos, sin = cos * step_c - sin * step_s, sin * step_c + cos * step_s
        return 0

    lax.fori_loop(0, 16, table_step, 0)

    vis_copy.wait()
    beam_copy = pltpu.make_async_copy(beam_hbm, beam, beam_sem)
    beam_copy.start()
    tail[...] = jnp.zeros(tail.shape, BF16)
    tail[:, pl.ds(0, PAIRS - WHOLE)] = vis[:, pl.ds(WHOLE, PAIRS - WHOLE)]

    lane = lax.broadcasted_iota(jnp.int32, (1, 128), 1)
    left = lane < B_BLK

    def chunk_step(k, _):
        batch = jnp.where(k >= 4, 1, 0)
        n = k - 4 * batch
        chips = []
        places = []
        for sub in range(4):
            dx = dy = 0
            for i in range(4):
                dx = jnp.where(n == i, OFFSETS[i][sub][0], dx)
                dy = jnp.where(n == i, OFFSETS[i][sub][1], dy)
            chips.append(wrap(y + dy, 4) * 4 + wrap(x + dx, 4))
            places.append(wrap(y + dy, 4) * 16 + half * 8 + wrap(x + dx, 4) * 2)
        wanted = jnp.full((1, PADDED), -1.0, F32)
        for sub in range(4):
            wanted = jnp.where(high[...] == batch * 16 + chips[sub], low[...] + (sub * B_BLK), wanted)
        rows = lax.broadcasted_iota(jnp.int32, (CHUNK, PADDED), 0).astype(BF16)
        one = jnp.where(rows == jnp.broadcast_to(wanted.astype(BF16), (CHUNK, PADDED)), BF16(1), BF16(0))
        sums = lax.dot_general(vis[:, pl.ds(0, WHOLE)], one[:, :WHOLE], NT, preferred_element_type=F32)
        sums += lax.dot_general(tail[...], one[:, WHOLE:], NT, preferred_element_type=F32)
        for pair in range(2):
            near, far = chips[pair * 2], chips[pair * 2 + 1]
            scale = 1.0 / jnp.where(left, counts[pl.ds(batch * 16 + near, 1), :], counts[pl.ds(batch * 16 + far, 1), :])
            for c in range(2):
                real = sums[c * 128 : c * 128 + T_BLK, pair * 128 : (pair + 1) * 128] * scale
                imag = sums[c * 128 + T_BLK : (c + 1) * 128, pair * 128 : (pair + 1) * 128] * scale
                s1[batch, near * 2 + c] = jnp.where(left, real, pltpu.roll(imag, B_BLK, 1)).astype(BF16)
                s1[batch, far * 2 + c] = jnp.where(left, pltpu.roll(real, B_BLK, 1), imag).astype(BF16)

        @pl.when(k == 0)
        def _():
            pl.semaphore_wait(barrier, HALF - 1 + 1 + 3)
            pl.semaphore_signal(z_sem, inc=1, device_id=(partner, af), device_id_type=MESH)

        for sub in range(4):
            for c in range(2):
                d = chips[sub] * 2 + c

                def send(d=d, to=places[sub] + c):
                    pltpu.make_async_remote_copy(
                        src_ref=s1.at[batch, d], dst_ref=r1.at[batch, g], send_sem=ss1, recv_sem=rs1.at[batch],
                        device_id=(to, af), device_id_type=MESH,
                    ).start()

                if sub < 3:
                    send()
                else:
                    pl.when(d != g)(send)

                    @pl.when(d == g)
                    def _():
                        pltpu.make_async_copy(s1.at[batch, d], r1.at[batch, d], rs1.at[batch]).start()

        return 0

    sign = jnp.where(left, 1.0, -1.0)
    upper = (lax.broadcasted_iota(jnp.int32, (1, 8, 1), 1)) < 4

    def gather(batch):
        part = r1.at[batch]
        pltpu.make_async_copy(part, part, rs1.at[batch]).wait()
        a = [r1[batch, q * 8 : (q + 1) * 8].reshape(8 * T_BLK, 2 * B_BLK).astype(F32) for q in range(4)]
        even, odd = a[0] + a[2], a[1] + a[3]
        series[batch, 0] = (even + odd).astype(BF16)
        series[batch, 2] = (even - odd).astype(BF16)
        even, odd = a[0] - a[2], sign * pltpu.roll(a[1] - a[3], B_BLK, 1)
        series[batch, 1] = (even + odd).astype(BF16)
        series[batch, 3] = (even - odd).astype(BF16)

    def transform(batch, own):
        both = []
        for k in range(4):
            along = jnp.dot(table[k, own], series[batch, k], preferred_element_type=F32)
            mixed = along[0:128] + sign * pltpu.roll(along[128:256], B_BLK, 1)
            both.append(mixed.reshape(HALF // 2, 8, 2 * B_BLK))
        for p in range(2):
            first, second = both[2 * p], both[2 * p + 1]
            now = jnp.where(upper, first, pltpu.roll(second, 4, 1))
            later = jnp.where(upper, pltpu.roll(first, 4, 1), second)
            halves[:, 0, p * 8 : (p + 1) * 8, :] = now
            halves[:, 1, p * 8 : (p + 1) * 8, :] = later
        s2[batch, own] = halves[...].reshape(HALF, SEG, 2 * B_BLK).astype(BF16)

    def send_spectra(batch, own):
        for dy in range(4):
            other = wrap(y + dy, 4)

            def send(k, _, other=other):
                near = wrap(place + k, 8)
                pltpu.make_async_remote_copy(
                    src_ref=s2.at[batch, own, other * 8 + near], dst_ref=r2.at[batch, ma], send_sem=ss2, recv_sem=rs2.at[batch, y],
                    device_id=(other * 16 + (half if own else 1 - half) * 8 + near, af), device_id_type=MESH,
                ).start()
                return 0

            lax.fori_loop(1 if own and not dy else 0, 8, send, 0)
        if own:
            pltpu.make_async_copy(s2.at[batch, 1, g], r2.at[batch, ma], rs2.at[batch, y]).start()

    lax.fori_loop(0, 8, chunk_step, 0)
    pl.semaphore_wait(z_sem, 1)
    gather(0)
    transform(0, 0)
    send_spectra(0, 0)
    transform(0, 1)
    gather(1)
    transform(1, 0)
    send_spectra(1, 0)
    send_spectra(0, 1)
    transform(1, 1)
    send_spectra(1, 1)
    kl_copy.wait()
    for m in range(4):
        turned_kl[m] = kl[m].T
    weights[...] = jnp.zeros(weights.shape, BF16)
    total[...] = jnp.zeros(total.shape, F32)
    v_send[...] = jnp.zeros(v_send.shape, F32)


    beam_copy.wait()

    def project_step(k, _):
        batch = jnp.where(k >= 4, 1, 0)
        q = wrap(y - (k - 4 * batch) + 4, 4)
        part = r2.at[batch, pl.ds(q * 16, 16)]
        pltpu.make_async_copy(part, part, rs2.at[batch, q]).wait()
        for c in range(2):
            for h in range(2):
                for pair in range(2):
                    near = r2[batch, q * 16 + h * 8 + pair * 4 + c].astype(F32)
                    far = r2[batch, q * 16 + h * 8 + pair * 4 + 2 + c].astype(F32)
                    real = jnp.where(left, near, pltpu.roll(far, B_BLK, 1))
                    imag = jnp.where(left, pltpu.roll(near, B_BLK, 1), far)
                    weights[c, h * 2 * SEG : (h * 2 + 1) * SEG, pair * 128 : (pair + 1) * 128] = real.astype(BF16)
                    weights[c, (h * 2 + 1) * SEG : (h * 2 + 2) * SEG, pair * 128 : (pair + 1) * 128] = imag.astype(BF16)
        column = pl.multiple_of(batch * 1024 + q * 256, 256)
        for c in range(2):
            total[c] += lax.dot_general(beam[c, :, pl.ds(column, 256)], weights[c], NT, preferred_element_type=F32)
        return 0

    lax.fori_loop(0, 8, project_step, 0)

    mode_lane = lax.broadcasted_iota(jnp.int32, (32, 128), 1)
    is_real = ((mode_lane >> 4) & 1) == 0
    mode_of = ((((mode_lane >> 2) & 3) - starts[ma]) & 3) + 4 * (mode_lane & 3)
    pieces = []
    for c in range(2):
        own = []
        for q in range(2):
            kept = jnp.zeros((32, 128), F32)
            for m in range(SEG):
                kept = jnp.where(mode_of == m, total[c, m * 64 + q * 32 : m * 64 + (q + 1) * 32, :], kept)
            own.append(kept)
        pieces.append(jnp.where(is_real, own[0], own[1]))
        pieces.append(jnp.where(is_real, -own[1], own[0]))
    turned = jnp.concatenate(pieces, axis=0).T
    sky = turned[0:16] + turned[16:32] + turned[32:48] + turned[48:64]
    window = jnp.full((4, 128), 0, jnp.int32) + starts[ma]
    for i in range(4):
        kept = sky[0:4]
        for k in range(1, 4):
            kept = jnp.where(((window + i) & 3) == k, sky[k * 4 : k * 4 + 4], kept)
        for n in range(4):
            v_send[n, i : i + 1, :] = kept[n : n + 1]
    pltpu.make_async_copy(v_send.at[af], v_recv.at[af], rsv).start()

    def send_sky(k, _):
        a = wrap(af + k, 4)
        pltpu.make_async_remote_copy(
            src_ref=v_send.at[a], dst_ref=v_recv.at[af], send_sem=ssv, recv_sem=rsv,
            device_id=(ma, a), device_id_type=MESH,
        ).start()
        return 0

    lax.fori_loop(1, 4, send_sky, 0)
    pltpu.make_async_copy(v_recv, v_recv, rsv).wait()
    vectors = (v_recv[0] + v_recv[1] + v_recv[2] + v_recv[3]).T
    for m in range(4):
        product = turned_kl[m] * jnp.broadcast_to(vectors[:, m : m + 1], (128, 128))
        out[m : m + 1, :] = jnp.sum(product, axis=0, keepdims=True)

    sent = s1.at[:, pl.ds(0, HALF - 1)]
    pltpu.make_async_copy(sent, sent, ss1).wait()
    for sent in (s2.at[:, 0], s2.at[:, 1, pl.ds(0, HALF - 1)]):
        pltpu.make_async_copy(sent, sent, ss2).wait()
    sent = v_send.at[pl.ds(0, 3)]
    pltpu.make_async_copy(sent, sent, ssv).wait()


def body(visibilities, pair_base, window_starts, beam, kl_basis):
    vis = visibilities.reshape(4 * T_BLK, PAIRS)
    rows = beam.reshape(2, SEG * 64, BASES)
    vmem = pl.BlockSpec(memory_space=pltpu.VMEM)
    return pl.pallas_call(
        kernel,
        out_shape=pltpu.VMEM((4, 128), F32),
        in_specs=[
            pl.BlockSpec(memory_space=pltpu.SMEM),
            vmem,
            pl.BlockSpec(memory_space=pl.ANY),
            pl.BlockSpec(memory_space=pl.ANY),
            pl.BlockSpec(memory_space=pl.ANY),
        ],
        out_specs=vmem,
        scratch_shapes=[
            pltpu.VMEM((4 * T_BLK, PAIRS), BF16),
            pltpu.VMEM((4 * T_BLK, PADDED - WHOLE), BF16),
            pltpu.VMEM((2, SEG * 64, BASES), BF16),
            pltpu.VMEM((1, PADDED), jnp.int32),
            pltpu.VMEM((1, PADDED), F32),
            pltpu.VMEM((32, 2 * B_BLK), F32),
            pltpu.VMEM((4, 2, 256, 512), BF16),
            pltpu.VMEM((2, HALF, T_BLK, 2 * B_BLK), BF16),
            pltpu.VMEM((2, HALF, T_BLK, 2 * B_BLK), BF16),
            pltpu.VMEM((2, 2, HALF, SEG, 2 * B_BLK), BF16),
            pltpu.VMEM((2, SEGS, SEG, 2 * B_BLK), BF16),
            pltpu.VMEM((2, 4, 512, 2 * B_BLK), BF16),
            pltpu.VMEM((HALF // 2, 2, SEG, 2 * B_BLK), F32),
            pltpu.VMEM((2, 128, 256), BF16),
            pltpu.VMEM((2, SEG * 64, 128), F32),
            pltpu.VMEM((4, 128, 128), F32),
            pltpu.VMEM((4, 128, 128), F32),
            pltpu.VMEM((4, 8, 128), F32),
            pltpu.VMEM((4, 8, 128), F32),
            pltpu.SemaphoreType.DMA,
            pltpu.SemaphoreType.DMA,
            pltpu.SemaphoreType.DMA,
            pltpu.SemaphoreType.DMA,
            pltpu.SemaphoreType.DMA((2,)),
            pltpu.SemaphoreType.DMA,
            pltpu.SemaphoreType.DMA((2, 4)),
            pltpu.SemaphoreType.REGULAR,
            pltpu.SemaphoreType.DMA,
            pltpu.SemaphoreType.DMA,
        ],
        compiler_params=pltpu.CompilerParams(
            collective_id=0, has_side_effects=True, vmem_limit_bytes=56 * 2**20
        ),
    )(window_starts, pair_base.reshape(1, PAIRS), kl_basis, vis, rows)


def solution(mesh):
    in_specs = (
        P(None, None, "ma", "af"),
        P("af"),
        P(),
        P(None, "ma", None, None, "af"),
        P(("ma", "af"), None, None),
    )
    out_specs = P(("ma", "af"), None)
    return jax.shard_map(body, mesh=mesh, in_specs=in_specs, out_specs=out_specs, check_vma=False)
```

```python
import math

import jax
import jax.numpy as jnp
from jax import lax
from jax.experimental import pallas as pl
from jax.experimental.pallas import tpu as pltpu
from jax.sharding import PartitionSpec as P

MESH = pl.DeviceIdType.MESH
F32 = jnp.float32
BF16 = jnp.bfloat16

TIMES = 4096
SEG = 16
SEGS = 64
PAIRS = 8160
PADDED = 8192
WHOLE = 7936
BASES = 2048
T_BLK = 64
HALF = 32
B_BLK = 64
CHUNK = 256
OFFSETS = (
    ((2, 1), (2, 3), (1, 2), (3, 2)),
    ((2, 0), (0, 2), (1, 1), (3, 3)),
    ((1, 3), (3, 1), (2, 2), (1, 0)),
    ((0, 1), (3, 0), (0, 3), (0, 0)),
)
NT = (((1,), (1,)), ((), ()))


def wrap(value, size):
    return jnp.where(value >= size, value - size, value)


def sincos(phase):
    quadrant = (phase + 512) >> 10
    x = (phase - (quadrant << 10)).astype(F32) * (2.0 * math.pi / TIMES)
    x2 = x * x
    s = x * (1.0 + x2 * (-1.0 / 6 + x2 * (1.0 / 120 + x2 * (-1.0 / 5040 + x2 * (1.0 / 362880)))))
    c = 1.0 + x2 * (-0.5 + x2 * (1.0 / 24 + x2 * (-1.0 / 720 + x2 * (1.0 / 40320))))
    odd = (quadrant & 1) == 1
    cos = jnp.where(odd, s, c)
    sin = jnp.where(odd, c, s)
    cos = jnp.where(((quadrant + 1) & 2) == 2, -cos, cos)
    sin = jnp.where((quadrant & 2) == 2, -sin, sin)
    return cos, sin


def kernel(
    starts, ids, kl_hbm, vis_hbm, beam_hbm, out,
    vis, tail, beam, high, low, counts, table, s1, r1, s2, r2, series, halves, weights, total, kl, turned_kl, v_send, v_recv,
    vis_sem, kl_sem, beam_sem, ss1, rs1, ss2, rs2, z_sem, ssv, rsv,
):
    ma = lax.axis_index("ma")
    af = lax.axis_index("af")
    y = ma // 16
    half = (ma // 8) % 2
    place = ma % 8
    g = y * 8 + place
    x = place // 2
    partner = ma + 8 - 16 * half

    vis_copy = pltpu.make_async_copy(vis_hbm, vis, vis_sem)
    vis_copy.start()
    kl_copy = pltpu.make_async_copy(kl_hbm, kl, kl_sem)
    kl_copy.start()

    barrier = pltpu.get_barrier_semaphore()
    pl.semaphore_signal(barrier, inc=1, device_id=(partner, af), device_id_type=MESH)

    for dy in range(4):

        def greet(k, _, base=wrap(y + dy, 4) * 16 + half * 8):
            pl.semaphore_signal(barrier, inc=1, device_id=(base + wrap(place + k, 8), af), device_id_type=MESH)
            return 0

        lax.fori_loop(0 if dy else 1, 8, greet, 0)

    def greet_af(k, _):
        pl.semaphore_signal(barrier, inc=1, device_id=(ma, wrap(af + k, 4)), device_id_type=MESH)
        return 0

    lax.fori_loop(1, 4, greet_af, 0)

    high[...] = jnp.full(high.shape, -1, jnp.int32)
    low[...] = jnp.zeros(low.shape, F32)
    local = ids[...] - af * BASES
    high[:, pl.ds(0, PAIRS)] = local >> 6
    low[:, pl.ds(0, PAIRS)] = (local & 63).astype(F32)
    rows_hi = lax.broadcasted_iota(jnp.int32, (32, PADDED), 0)
    rows_lo = (lax.broadcasted_iota(jnp.int32, (2 * B_BLK, PADDED), 0) & (B_BLK - 1)).astype(BF16)
    one_hi = jnp.where(rows_hi == jnp.broadcast_to(high[...], (32, PADDED)), 1.0, 0.0).astype(BF16)
    one_lo = jnp.where(rows_lo == jnp.broadcast_to(low[...].astype(BF16), (2 * B_BLK, PADDED)), BF16(1), BF16(0))
    counts[...] = lax.dot_general(one_hi, one_lo, NT, preferred_element_type=F32)

    lanes = lax.broadcasted_iota(jnp.int32, (SEG, 128), 1)
    within = lax.broadcasted_iota(jnp.int32, (SEG, 128), 0)
    window_row = within >> 2
    first_time = lanes + half * 512
    turns = []
    for b in range(4):
        up = sincos((first_time + 128 * b) & (TIMES - 1))
        down = sincos((-3 * (first_time + 128 * b)) & (TIMES - 1))
        turns.append((up, down))

    def table_step(tile, _):
        start = jnp.full((SEG, 128), 0, jnp.int32)
        for w in range(4):
            start = jnp.where(window_row == w, starts[tile * 4 + w], start)
        mode = start + ((-start) & 3) + 4 * (within & 3)
        cos, sin = sincos((first_time * mode) & (TIMES - 1))
        cos = cos * (1.0 / math.sqrt(TIMES))
        sin = sin * (1.0 / math.sqrt(TIMES))
        step_c, step_s = sincos((128 * mode) & (TIMES - 1))
        own = jnp.where((tile // 2) % 2 == half, 1, 0)
        row = pl.multiple_of((tile // 4 * 2 + tile % 2) * SEG, SEG)
        wraps = [((k - start) & 3) == 0 for k in range(4)]
        for b in range(4):
            c, d = cos, sin
            for k in range(4):
                if k:
                    (up_c, up_s), (down_c, down_s) = turns[b]
                    turn_c = jnp.where(wraps[k], down_c, up_c)
                    turn_s = jnp.where(wraps[k], down_s, up_s)
                    c, d = c * turn_c - d * turn_s, d * turn_c + c * turn_s
                table[k, own, pl.ds(row, SEG), b * 128 : (b + 1) * 128] = c.astype(BF16)
                table[k, own, pl.ds(row + 128, SEG), b * 128 : (b + 1) * 128] = d.astype(BF16)
            if b < 3:
                cos, sin = cos * step_c - sin * step_s, sin * step_c + cos * step_s
        return 0

    lax.fori_loop(0, 16, table_step, 0)

    vis_copy.wait()
    beam_copy = pltpu.make_async_copy(beam_hbm, beam, beam_sem)
    beam_copy.start()
    tail[...] = jnp.zeros(tail.shape, BF16)
    tail[:, pl.ds(0, PAIRS - WHOLE)] = vis[:, pl.ds(WHOLE, PAIRS - WHOLE)]

    lane = lax.broadcasted_iota(jnp.int32, (1, 128), 1)
    left = lane < B_BLK

    def chunk_step(k, _):
        batch = jnp.where(k >= 4, 1, 0)
        n = k - 4 * batch
        chips = []
        places = []
        for sub in range(4):
            dx = dy = 0
            for i in range(4):
                dx = jnp.where(n == i, OFFSETS[i][sub][0], dx)
                dy = jnp.where(n == i, OFFSETS[i][sub][1], dy)
            chips.append(wrap(y + dy, 4) * 4 + wrap(x + dx, 4))
            places.append(wrap(y + dy, 4) * 16 + half * 8 + wrap(x + dx, 4) * 2)
        wanted = jnp.full((1, PADDED), -1.0, F32)
        for sub in range(4):
            wanted = jnp.where(high[...] == batch * 16 + chips[sub], low[...] + (sub * B_BLK), wanted)
        rows = lax.broadcasted_iota(jnp.int32, (CHUNK, PADDED), 0).astype(BF16)
        one = jnp.where(rows == jnp.broadcast_to(wanted.astype(BF16), (CHUNK, PADDED)), BF16(1), BF16(0))
        pairs = jnp.concatenate([vis[:, pl.ds(0, WHOLE)], tail[...]], axis=1)
        sums = lax.dot_general(pairs, one, NT, preferred_element_type=F32)
        for pair in range(2):
            near, far = chips[pair * 2], chips[pair * 2 + 1]
            scale = 1.0 / jnp.where(left, counts[pl.ds(batch * 16 + near, 1), :], counts[pl.ds(batch * 16 + far, 1), :])
            for c in range(2):
                real = sums[c * 128 : c * 128 + T_BLK, pair * 128 : (pair + 1) * 128] * scale
                imag = sums[c * 128 + T_BLK : (c + 1) * 128, pair * 128 : (pair + 1) * 128] * scale
                s1[batch, near * 2 + c] = jnp.where(left, real, pltpu.roll(imag, B_BLK, 1)).astype(BF16)
                s1[batch, far * 2 + c] = jnp.where(left, pltpu.roll(real, B_BLK, 1), imag).astype(BF16)

        @pl.when(k == 0)
        def _():
            pl.semaphore_wait(barrier, HALF - 1 + 1 + 3)
            pl.semaphore_signal(z_sem, inc=1, device_id=(partner, af), device_id_type=MESH)

        for sub in range(4):
            for c in range(2):
                d = chips[sub] * 2 + c

                def send(d=d, to=places[sub] + c):
                    pltpu.make_async_remote_copy(
                        src_ref=s1.at[batch, d], dst_ref=r1.at[batch, g], send_sem=ss1, recv_sem=rs1.at[batch],
                        device_id=(to, af), device_id_type=MESH,
                    ).start()

                if sub < 3:
                    send()
                else:
                    pl.when(d != g)(send)

                    @pl.when(d == g)
                    def _():
                        pltpu.make_async_copy(s1.at[batch, d], r1.at[batch, d], rs1.at[batch]).start()

        return 0

    sign = jnp.where(left, 1.0, -1.0)
    upper = (lax.broadcasted_iota(jnp.int32, (1, 8, 1), 1)) < 4

    def gather(batch):
        part = r1.at[batch]
        pltpu.make_async_copy(part, part, rs1.at[batch]).wait()
        a = [r1[batch, q * 8 : (q + 1) * 8].reshape(8 * T_BLK, 2 * B_BLK).astype(F32) for q in range(4)]
        even, odd = a[0] + a[2], a[1] + a[3]
        series[batch, 0] = (even + odd).astype(BF16)
        series[batch, 2] = (even - odd).astype(BF16)
        even, odd = a[0] - a[2], sign * pltpu.roll(a[1] - a[3], B_BLK, 1)
        series[batch, 1] = (even + odd).astype(BF16)
        series[batch, 3] = (even - odd).astype(BF16)

    def transform(batch, own):
        both = []
        for k in range(4):
            along = jnp.dot(table[k, own], series[batch, k], preferred_element_type=F32)
            mixed = along[0:128] + sign * pltpu.roll(along[128:256], B_BLK, 1)
            both.append(mixed.reshape(HALF // 2, 8, 2 * B_BLK))
        for p in range(2):
            first, second = both[2 * p], both[2 * p + 1]
            now = jnp.where(upper, first, pltpu.roll(second, 4, 1))
            later = jnp.where(upper, pltpu.roll(first, 4, 1), second)
            halves[:, 0, p * 8 : (p + 1) * 8, :] = now
            halves[:, 1, p * 8 : (p + 1) * 8, :] = later
        s2[batch, own] = halves[...].reshape(HALF, SEG, 2 * B_BLK).astype(BF16)

    def send_spectra(batch, own):
        for dy in range(4):
            other = wrap(y + dy, 4)

            def send(k, _, other=other):
                near = wrap(place + k, 8)
                pltpu.make_async_remote_copy(
                    src_ref=s2.at[batch, own, other * 8 + near], dst_ref=r2.at[batch, ma], send_sem=ss2, recv_sem=rs2.at[batch, y],
                    device_id=(other * 16 + (half if own else 1 - half) * 8 + near, af), device_id_type=MESH,
                ).start()
                return 0

            lax.fori_loop(1 if own and not dy else 0, 8, send, 0)
        if own:
            pltpu.make_async_copy(s2.at[batch, 1, g], r2.at[batch, ma], rs2.at[batch, y]).start()

    lax.fori_loop(0, 8, chunk_step, 0)
    pl.semaphore_wait(z_sem, 1)
    gather(0)
    transform(0, 0)
    send_spectra(0, 0)
    transform(0, 1)
    gather(1)
    transform(1, 0)
    send_spectra(1, 0)
    send_spectra(0, 1)
    transform(1, 1)
    send_spectra(1, 1)
    kl_copy.wait()
    for m in range(4):
        turned_kl[m] = kl[m].T
    weights[...] = jnp.zeros(weights.shape, BF16)
    total[...] = jnp.zeros(total.shape, F32)
    v_send[...] = jnp.zeros(v_send.shape, F32)


    beam_copy.wait()

    def project_step(k, _):
        batch = jnp.where(k >= 4, 1, 0)
        q = wrap(y - (k - 4 * batch) + 4, 4)
        part = r2.at[batch, pl.ds(q * 16, 16)]
        pltpu.make_async_copy(part, part, rs2.at[batch, q]).wait()
        for c in range(2):
            for h in range(2):
                for pair in range(2):
                    near = r2[batch, q * 16 + h * 8 + pair * 4 + c].astype(F32)
                    far = r2[batch, q * 16 + h * 8 + pair * 4 + 2 + c].astype(F32)
                    real = jnp.where(left, near, pltpu.roll(far, B_BLK, 1))
                    imag = jnp.where(left, pltpu.roll(near, B_BLK, 1), far)
                    weights[c, h * 2 * SEG : (h * 2 + 1) * SEG, pair * 128 : (pair + 1) * 128] = real.astype(BF16)
                    weights[c, (h * 2 + 1) * SEG : (h * 2 + 2) * SEG, pair * 128 : (pair + 1) * 128] = imag.astype(BF16)
        column = pl.multiple_of(batch * 1024 + q * 256, 256)
        for c in range(2):
            total[c] += lax.dot_general(beam[c, :, pl.ds(column, 256)], weights[c], NT, preferred_element_type=F32)
        return 0

    lax.fori_loop(0, 8, project_step, 0)

    mode_lane = lax.broadcasted_iota(jnp.int32, (32, 128), 1)
    is_real = ((mode_lane >> 4) & 1) == 0
    mode_of = ((((mode_lane >> 2) & 3) - starts[ma]) & 3) + 4 * (mode_lane & 3)
    pieces = []
    for c in range(2):
        own = []
        for q in range(2):
            kept = jnp.zeros((32, 128), F32)
            for m in range(SEG):
                kept = jnp.where(mode_of == m, total[c, m * 64 + q * 32 : m * 64 + (q + 1) * 32, :], kept)
            own.append(kept)
        pieces.append(jnp.where(is_real, own[0], own[1]))
        pieces.append(jnp.where(is_real, -own[1], own[0]))
    turned = jnp.concatenate(pieces, axis=0).T
    sky = turned[0:16] + turned[16:32] + turned[32:48] + turned[48:64]
    window = jnp.full((4, 128), 0, jnp.int32) + starts[ma]
    for i in range(4):
        kept = sky[0:4]
        for k in range(1, 4):
            kept = jnp.where(((window + i) & 3) == k, sky[k * 4 : k * 4 + 4], kept)
        for n in range(4):
            v_send[n, i : i + 1, :] = kept[n : n + 1]
    pltpu.make_async_copy(v_send.at[af], v_recv.at[af], rsv).start()

    def send_sky(k, _):
        a = wrap(af + k, 4)
        pltpu.make_async_remote_copy(
            src_ref=v_send.at[a], dst_ref=v_recv.at[af], send_sem=ssv, recv_sem=rsv,
            device_id=(ma, a), device_id_type=MESH,
        ).start()
        return 0

    lax.fori_loop(1, 4, send_sky, 0)
    pltpu.make_async_copy(v_recv, v_recv, rsv).wait()
    vectors = (v_recv[0] + v_recv[1] + v_recv[2] + v_recv[3]).T
    for m in range(4):
        product = turned_kl[m] * jnp.broadcast_to(vectors[:, m : m + 1], (128, 128))
        out[m : m + 1, :] = jnp.sum(product, axis=0, keepdims=True)

    sent = s1.at[:, pl.ds(0, HALF - 1)]
    pltpu.make_async_copy(sent, sent, ss1).wait()
    for sent in (s2.at[:, 0], s2.at[:, 1, pl.ds(0, HALF - 1)]):
        pltpu.make_async_copy(sent, sent, ss2).wait()
    sent = v_send.at[pl.ds(0, 3)]
    pltpu.make_async_copy(sent, sent, ssv).wait()


def body(visibilities, pair_base, window_starts, beam, kl_basis):
    vis = visibilities.reshape(4 * T_BLK, PAIRS)
    rows = beam.reshape(2, SEG * 64, BASES)
    vmem = pl.BlockSpec(memory_space=pltpu.VMEM)
    return pl.pallas_call(
        kernel,
        out_shape=pltpu.VMEM((4, 128), F32),
        in_specs=[
            pl.BlockSpec(memory_space=pltpu.SMEM),
            vmem,
            pl.BlockSpec(memory_space=pl.ANY),
            pl.BlockSpec(memory_space=pl.ANY),
            pl.BlockSpec(memory_space=pl.ANY),
        ],
        out_specs=vmem,
        scratch_shapes=[
            pltpu.VMEM((4 * T_BLK, PAIRS), BF16),
            pltpu.VMEM((4 * T_BLK, PADDED - WHOLE), BF16),
            pltpu.VMEM((2, SEG * 64, BASES), BF16),
            pltpu.VMEM((1, PADDED), jnp.int32),
            pltpu.VMEM((1, PADDED), F32),
            pltpu.VMEM((32, 2 * B_BLK), F32),
            pltpu.VMEM((4, 2, 256, 512), BF16),
            pltpu.VMEM((2, HALF, T_BLK, 2 * B_BLK), BF16),
            pltpu.VMEM((2, HALF, T_BLK, 2 * B_BLK), BF16),
            pltpu.VMEM((2, 2, HALF, SEG, 2 * B_BLK), BF16),
            pltpu.VMEM((2, SEGS, SEG, 2 * B_BLK), BF16),
            pltpu.VMEM((2, 4, 512, 2 * B_BLK), BF16),
            pltpu.VMEM((HALF // 2, 2, SEG, 2 * B_BLK), F32),
            pltpu.VMEM((2, 128, 256), BF16),
            pltpu.VMEM((2, SEG * 64, 128), F32),
            pltpu.VMEM((4, 128, 128), F32),
            pltpu.VMEM((4, 128, 128), F32),
            pltpu.VMEM((4, 8, 128), F32),
            pltpu.VMEM((4, 8, 128), F32),
            pltpu.SemaphoreType.DMA,
            pltpu.SemaphoreType.DMA,
            pltpu.SemaphoreType.DMA,
            pltpu.SemaphoreType.DMA,
            pltpu.SemaphoreType.DMA((2,)),
            pltpu.SemaphoreType.DMA,
            pltpu.SemaphoreType.DMA((2, 4)),
            pltpu.SemaphoreType.REGULAR,
            pltpu.SemaphoreType.DMA,
            pltpu.SemaphoreType.DMA,
        ],
        compiler_params=pltpu.CompilerParams(
            collective_id=0, has_side_effects=True, vmem_limit_bytes=56 * 2**20
        ),
    )(window_starts, pair_base.reshape(1, PAIRS), kl_basis, vis, rows)


def solution(mesh):
    in_specs = (
        P(None, None, "ma", "af"),
        P("af"),
        P(),
        P(None, "ma", None, None, "af"),
        P(("ma", "af"), None, None),
    )
    out_specs = P(("ma", "af"), None)
    return jax.shard_map(body, mesh=mesh, in_specs=in_specs, out_specs=out_specs, check_vma=False)
```
